32 devices in a mesh: rep: 2 (over y), mem: 4 (over x, core), tp: 4 (over z).
Axes of the slice: x: 2, y: 2, z: 4, core: 2. Of those that a mesh axis runs over, the one named last changes fastest.
Arguments:
- activations: bfloat16 [4096, 8192], P(('rep', 'mem'), 'tp'), parts along dimension 0, may hold values from -6 to 6
- base_weight: bfloat16 [8192, 1024], P('tp'), may hold values from -0.0625 to 0.0625
- pool_shrink: bfloat16 [128, 64, 8192], P('mem', None, 'tp'), may hold values from -0.0625 to 0.0625
- pool_expand: bfloat16 [128, 65536], P('mem', 'tp'), may hold values from -0.75 to 0.75
- cache_shrink: bfloat16 [32, 64, 8192], P(('rep', 'mem'), None, 'tp'), parts along dimension 0, may hold values from -0.0625 to 0.0625
- cache_expand: bfloat16 [32, 65536], P(('rep', 'mem'), 'tp'), parts along dimension 0, may hold values from -0.75 to 0.75
- adapter_home: int32 [256], P('rep'), parts along dimension 0, may hold values from 0 to 127, as said below
- evict_adapters: int32 [8, 2], P('rep'), parts along dimension 0, may hold values from 0 to 127, as said below
- evict_slots: int32 [8, 2], P(('rep', 'mem')), parts along dimension 0, may hold values from 0 to 3, as said below
- block_slot: int32 [32], P(('rep', 'mem')), parts along dimension 0, may hold values from 0 to 3, as said below
- block_live_rows: int32 [32], P(('rep', 'mem')), parts along dimension 0, may hold values from 32 to 128, as said below
Outputs:
- kv_out: bfloat16 [4096, 1024], P(('rep', 'mem', 'tp')), parts along dimension 0
The draws below stay inside these ranges and needn't reach their ends.
There are 2 independent parts, one for each index of `rep`. The reference program is written for one: setup_inputs(seed, part) draws one part's arguments, and reference() takes and returns one part's arrays. A program takes and returns all parts, laid end to end along the dimension named above; an argument that names none is the same for every part. Nothing has to cross between parts.
Inputs may be any that keep to these rules, and one draw needn't show every extreme that they name: `adapter_home`: a permutation of the pool rows. `evict_adapters`: an adapter a lies on pool device adapter_home[a] // 32; at most 1 of one group's loads lie on one pool device, and every group has exactly 1 on each device that it loads from. `evict_slots`: a group's 2 slots are distinct. `block_slot`: each group's 4 blocks use each of its slots once. `block_live_rows`: some block is full.
All inputs are finite; a program needn't handle non-finite values.
Results may differ from the reference program's by a relative error of at most 0.0029.
Values may be sent and summed in bfloat16 or wider, within the bound.
A program may use at most 64 MiB of HBM per device.

```python
import jax
import jax.numpy as jnp
from jax import lax

D = 8192
VALUE_FEATURES = 1024
R = 64
BLOCK = 128
POOL_DEV = 32
BLOCKS = 4
SLOTS = 4
EVICT = 2
ROWS = 2048
POOL = 128
N_MEM = 4


def pool_order(key):
    return jax.random.permutation(jax.random.fold_in(key, 11), POOL)


def draw_adapter_home(key, part):
    order = pool_order(key)
    return jnp.argsort(order, stable=True).astype(jnp.int32)


def draw_evict_adapters(key, part):
    order = pool_order(key)
    key = jax.random.fold_in(key, 3)
    first, second = jax.random.split(key, 2)
    start = jax.random.randint(first, (N_MEM, 1), 0, N_MEM)
    column = jnp.arange(EVICT)[None, :]
    owner = (start + column) % N_MEM
    local = jax.random.randint(second, (N_MEM, EVICT), 0, POOL_DEV)
    return order[owner * POOL_DEV + local].astype(jnp.int32)


def draw_evict_slots(key, part):
    key = jax.random.fold_in(key, 5)
    keys = jax.random.split(key, N_MEM)
    return jax.vmap(lambda single: jax.random.permutation(single, SLOTS)[:EVICT])(keys).astype(jnp.int32)


def draw_block_slot(key, part):
    key = jax.random.fold_in(key, 7)
    keys = jax.random.split(key, N_MEM)
    return jax.vmap(lambda single: jax.random.permutation(single, SLOTS))(keys).reshape(-1).astype(jnp.int32)


def draw_block_live_rows(key, part):
    key = jax.random.fold_in(key, 9)
    first, second = jax.random.split(key)
    count = N_MEM * BLOCKS
    values = jax.random.randint(first, (count,), BLOCK // 4, BLOCK + 1)
    spot = jax.random.randint(second, (), 0, count)
    index = jnp.arange(count)
    values = jnp.where(index == spot, BLOCK, values)
    values = jnp.where(index == (spot + 1) % count, BLOCK // 4, values)
    return values.astype(jnp.int32)


def steps_of(rng, shape, cuts, smallest, high):
    gain = 1.0
    for axis_at, parts in cuts:
        draws = jax.random.uniform(jax.random.fold_in(jax.random.fold_in(rng, 6), axis_at), (parts,), jnp.float32, smallest / len(cuts), high / len(cuts))
        gain = gain * jnp.repeat(jnp.exp(draws), shape[axis_at] // parts).reshape((-1,) + (1,) * (len(shape) - 1 - axis_at))
    return gain


def bell_draw(own_key, extent, scale, most, shards=(), kind=jnp.bfloat16):
    array = jax.random.normal(own_key, extent, jnp.float32) * scale
    if len(shards) > 0:
        array = steps_of(own_key, extent, shards, -0.22, 0.18) * array
    return jnp.clip(array, min=-most, max=most).astype(kind)


def setup_inputs(seed: int = 0, part: int = 0) -> dict:
    key_list = jax.random.split(jax.random.key(seed), 12)
    own_keys = jax.random.split(jax.random.fold_in(key_list[11], part), 12)
    return {
        "activations": bell_draw(own_keys[0], (ROWS, D), 1.0, 6.0, ((0, 4), (1, 4))),
        "base_weight": bell_draw(key_list[1], (D, VALUE_FEATURES), D ** -0.5, 0.0625, ((0, 4),)),
        "pool_shrink": bell_draw(key_list[2], (POOL, R, D), D ** -0.5, 0.0625, ((0, 4), (2, 4))),
        "pool_expand": bell_draw(key_list[3], (POOL, R * VALUE_FEATURES), R ** -0.5, 0.75, ((0, 4), (1, 4))),
        "cache_shrink": bell_draw(own_keys[4], (N_MEM * SLOTS, R, D), D ** -0.5, 0.0625, ((0, 4), (2, 4))),
        "cache_expand": bell_draw(own_keys[5], (N_MEM * SLOTS, R * VALUE_FEATURES), R ** -0.5, 0.75, ((0, 4), (1, 4))),
        "adapter_home": draw_adapter_home(jax.random.fold_in(jax.random.fold_in(key_list[11], part), 71), part),
        "evict_adapters": draw_evict_adapters(jax.random.fold_in(jax.random.fold_in(key_list[11], part), 71), part),
        "evict_slots": draw_evict_slots(jax.random.fold_in(jax.random.fold_in(key_list[11], part), 71), part),
        "block_slot": draw_block_slot(jax.random.fold_in(jax.random.fold_in(key_list[11], part), 71), part),
        "block_live_rows": draw_block_live_rows(jax.random.fold_in(jax.random.fold_in(key_list[11], part), 71), part),
    }


def reference(activations, base_weight, pool_shrink, pool_expand, cache_shrink, cache_expand, adapter_home, evict_adapters, evict_slots, block_slot, block_live_rows):
    groups = evict_slots.shape[0]
    pool_row = adapter_home[evict_adapters]
    group_ids = jnp.arange(groups, dtype=jnp.int32)[:, None]
    slot_shrink = cache_shrink.reshape(groups, SLOTS, R, D).at[group_ids, evict_slots].set(pool_shrink[pool_row])
    slot_expand = cache_expand.reshape(groups, SLOTS, R * VALUE_FEATURES).at[group_ids, evict_slots].set(pool_expand[pool_row])
    nblocks = block_slot.shape[0]
    block_group = jnp.arange(nblocks, dtype=jnp.int32) // BLOCKS
    block_shrink = slot_shrink[block_group, block_slot].astype(jnp.float32)
    block_expand_weight = slot_expand[block_group, block_slot].reshape(nblocks, R, VALUE_FEATURES).astype(jnp.float32)
    blocked = activations.reshape(nblocks, BLOCK, D).astype(jnp.float32)
    lowrank_state = jnp.einsum("nbd,nrd->nbr", blocked, block_shrink).astype(jnp.bfloat16)
    lowrank_state = lax.optimization_barrier(lowrank_state)
    adapter_output = jnp.einsum("daj,djz->daz", lowrank_state.astype(jnp.float32), block_expand_weight).reshape(-1, VALUE_FEATURES)
    base_output = jnp.dot(activations, base_weight, preferred_element_type=jnp.float32)
    position = jnp.arange(BLOCK, dtype=jnp.int32)[None, :]
    live_rows = (position < block_live_rows[:, None]).reshape(-1)
    return jnp.where(live_rows[:, None], base_output + 0.5 * adapter_output, 0.0).astype(jnp.bfloat16)
```

```python
import functools

import jax
import jax.numpy as jnp
from jax import lax
from jax.experimental import pallas as pl
from jax.experimental.pallas import tpu as pltpu
from jax.sharding import PartitionSpec as P

VALUE_FEATURES = 1024
BLOCK = 128
CAP = 1
SLOTS = 4
EVICT = 2


def plain_body(
    activations,
    base_weight,
    pool_shrink,
    pool_expand,
    cache_shrink,
    cache_expand,
    adapter_home,
    evict_adapters,
    evict_slots,
    block_slot,
    block_live_rows,
):
    groups = lax.axis_size("mem")
    tp_count = lax.axis_size("tp")
    group_index = lax.axis_index("mem")
    pool_dev = pool_shrink.shape[0]
    home = adapter_home[evict_adapters]
    owner = home // pool_dev
    position = jnp.arange(EVICT, dtype=jnp.int32)
    same = owner[:, :, None] == owner[:, None, :]
    earlier = position[None, None, :] < position[None, :, None]
    rank = jnp.sum((same & earlier).astype(jnp.int32), axis=2)
    local_row = home - owner * pool_dev
    wanted = (owner == group_index)[:, None, :] & (
        rank[:, None, :] == jnp.arange(CAP, dtype=jnp.int32)[None, :, None]
    )
    send_row = jnp.sum(jnp.where(wanted, local_row[:, None, :], 0), axis=2)
    got_shrink, got_expand = (
        lax.all_to_all(pool_shrink[send_row], "mem", split_axis=0, concat_axis=0, tiled=True),
        lax.all_to_all(pool_expand[send_row], "mem", split_axis=0, concat_axis=0, tiled=True),
    )
    my_owner = lax.dynamic_index_in_dim(owner, group_index, 0, keepdims=False)
    my_rank = lax.dynamic_index_in_dim(rank, group_index, 0, keepdims=False)
    flat = my_owner * CAP + my_rank
    new_shrink = got_shrink.reshape((groups * CAP,) + got_shrink.shape[2:])[flat]
    new_expand = got_expand.reshape(groups * CAP, got_expand.shape[2])[flat]
    targets = evict_slots[0]
    slot_shrink = cache_shrink.at[targets].set(new_shrink)
    slot_expand = cache_expand.at[targets].set(new_expand)
    rows = activations.shape[0]
    nblocks = rows // BLOCK
    blocked = activations.reshape(nblocks, BLOCK, activations.shape[1])
    lowrank_state = jnp.einsum(
        "nbd,nrd->nbr", blocked, slot_shrink[block_slot], preferred_element_type=jnp.float32
    ).reshape(rows, -1)
    row_ids = jnp.arange(rows, dtype=jnp.int32)
    block_hot = (row_ids // BLOCK)[:, None] == jnp.arange(nblocks, dtype=jnp.int32)[None, :]
    row_slot = jnp.sum(jnp.where(block_hot, block_slot[None, :], 0), axis=1)
    row_live = row_ids % BLOCK < jnp.sum(jnp.where(block_hot, block_live_rows[None, :], 0), axis=1)
    slot_hot = row_slot[:, None] == jnp.arange(SLOTS, dtype=jnp.int32)[None, :]
    own = rows // tp_count
    start = lax.axis_index("tp") * own
    zero_value = jnp.zeros((), jnp.bfloat16)
    base_rows = lax.psum_scatter(
        jnp.dot(activations, base_weight, preferred_element_type=jnp.float32),
        "tp",
        scatter_dimension=0,
        tiled=True,
    )
    low_rows = lax.psum_scatter(lowrank_state, "tp", scatter_dimension=0, tiled=True).astype(
        jnp.bfloat16
    )
    full_expand = lax.all_gather(slot_expand, "tp", axis=1, tiled=True).reshape(-1, VALUE_FEATURES)
    own_hot = lax.dynamic_slice_in_dim(slot_hot, start, own, 0)
    chosen = jnp.where(own_hot[:, :, None], low_rows[:, None, :], zero_value).reshape(own, -1)
    total = base_rows + 0.5 * jnp.dot(chosen, full_expand, preferred_element_type=jnp.float32)
    own_live = lax.dynamic_slice_in_dim(row_live, start, own, 0)
    return jnp.where(own_live[:, None], total, 0.0).astype(jnp.bfloat16)


CHUNKS = 4
MESH = pl.DeviceIdType.MESH


def kernel(
    nm, nt, act_h, w_h, psh_h, pex_h, csh_h, cex_h, home, evict, eslot, bslot, live,
    out,
    act, w, psh, pst, allsh, alle, ssh, sex, xe, full, pf, own, sb, rb, slow, rlow,
    loc, pex_sem, s_base, r_base, s_sh, r_sh, s_ex, r_ex, s_xe, r_xe, s_low, r_low,
):
    mm = lax.axis_index("mem")
    mt = lax.axis_index("tp")
    pool_dev = psh_h.shape[0]
    ranks = cex_h.shape[1]
    wide = w_h.shape[1] // CHUNKS

    barrier = pltpu.get_barrier_semaphore()
    for k in range(1, nt):
        pl.semaphore_signal(barrier, inc=1, device_id={"tp": lax.rem(mt + k, nt)}, device_id_type=MESH)
    for k in range(1, nm):
        pl.semaphore_signal(barrier, inc=1, device_id={"mem": lax.rem(mm + k, nm)}, device_id_type=MESH)

    load_act = pltpu.make_async_copy(act_h, act, loc.at[0])
    load_act.start()
    load_w = []
    for c in range(CHUNKS):
        load_w.append(pltpu.make_async_copy(w_h.at[:, pl.ds(c * wide, wide)], w.at[c], loc.at[1 + c]))
        load_w[c].start()
    load_pex = []
    for r in range(ranks):
        load_pex.append(pltpu.make_async_copy(
            pex_h.at[:, pl.ds(r * VALUE_FEATURES, VALUE_FEATURES)],
            pst.at[pl.ds(r * pool_dev, pool_dev), :],
            pex_sem.at[r],
        ))
        load_pex[r].start()
    load_psh = pltpu.make_async_copy(psh_h, psh, loc.at[5])
    load_psh.start()
    load_csh = pltpu.make_async_copy(csh_h, allsh.at[pl.ds(0, SLOTS)], loc.at[6])
    load_csh.start()
    load_cex = pltpu.make_async_copy(cex_h, alle.at[pl.ds(0, SLOTS)], loc.at[7])
    load_cex.start()

    def base_copy(c, peer, slot):
        return pltpu.make_async_remote_copy(
            src_ref=sb.at[c, peer], dst_ref=rb.at[c, slot],
            send_sem=s_base.at[c, peer], recv_sem=r_base.at[c, slot],
            device_id={"tp": peer}, device_id_type=MESH)

    def pair_copy(a, b, ss, rs, axis, peer, slot, base=0):
        return pltpu.make_async_remote_copy(
            src_ref=a.at[peer], dst_ref=b.at[base + slot],
            send_sem=ss.at[peer], recv_sem=rs.at[slot],
            device_id={axis: peer}, device_id_type=MESH)

    load_act.wait()
    for c in range(CHUNKS):
        load_w[c].wait()
        pf[...] = jnp.dot(act[...], w[c], preferred_element_type=jnp.float32)
        if c == 0:
            pl.semaphore_wait(barrier, nt - 1 + nm - 1)
        for k in range(1, nt):
            peer = lax.rem(mt + k, nt)
            sb[c, peer] = pf[pl.ds(pl.multiple_of(peer * BLOCK, BLOCK), BLOCK), :].astype(jnp.bfloat16)
            base_copy(c, peer, mt).start()
        own[:, c * wide:(c + 1) * wide] = pf[pl.ds(pl.multiple_of(mt * BLOCK, BLOCK), BLOCK), :]

    def wanted(g):
        row = jnp.int32(0)
        for e in range(EVICT):
            h = home[evict[g, e]]
            o = lax.div(h, jnp.int32(pool_dev))
            row = jnp.where(o == mm, h - o * pool_dev, row)
        return row

    rows = [wanted(g) for g in range(nm)]
    shape = (nm * ranks, ranks * pool_dev)
    i = lax.broadcasted_iota(jnp.int32, shape, 0)
    q = lax.broadcasted_iota(jnp.int32, shape, 1)
    target = jnp.zeros(shape, jnp.int32)
    for g in range(nm):
        target = jnp.where((i >= g * ranks) & (i < (g + 1) * ranks), (i - g * ranks) * pool_dev + rows[g], target)
    hot = jnp.where(q == target, 1.0, 0.0).astype(jnp.bfloat16)
    for r in range(ranks):
        load_pex[r].wait()
    picked = jnp.dot(hot, pst[...], preferred_element_type=jnp.float32).astype(jnp.bfloat16)
    sex[...] = picked.reshape(nm, ranks, VALUE_FEATURES)
    for k in range(1, nm):
        pair_copy(sex, alle, s_ex, r_ex, "mem", lax.rem(mm + k, nm), mm, SLOTS).start()
    alle[SLOTS + mm] = sex[mm]
    load_psh.wait()
    for k in range(1, nm):
        g = lax.rem(mm + k, nm)
        ssh[g] = psh[wanted(g)]
        pair_copy(ssh, allsh, s_sh, r_sh, "mem", g, mm, SLOTS).start()
    allsh[SLOTS + mm] = psh[wanted(mm)]

    owner = [lax.div(home[evict[mm, e]], jnp.int32(pool_dev)) for e in range(EVICT)]

    def place(b):
        c = bslot[b]
        index = c
        for e in range(EVICT):
            index = jnp.where(eslot[0, e] == c, SLOTS + owner[e], index)
        return index

    load_cex.wait()
    for k in range(1, nm):
        pair_copy(sex, alle, s_ex, r_ex, "mem", lax.rem(mm + k, nm), lax.rem(mm + k, nm), SLOTS).wait_recv()
    for k in range(1, nt):
        peer = lax.rem(mt + k, nt)
        xe[peer] = alle[place(peer)]
        pair_copy(xe, full, s_xe, r_xe, "tp", peer, mt).start()
    full[mt] = alle[place(mt)]

    load_csh.wait()
    for k in range(1, nm):
        pair_copy(ssh, allsh, s_sh, r_sh, "mem", lax.rem(mm + k, nm), lax.rem(mm + k, nm), SLOTS).wait_recv()

    def low_of(b):
        return lax.dot_general(
            allsh[place(b)], act[pl.ds(pl.multiple_of(b * BLOCK, BLOCK), BLOCK), :],
            (((1,), (1,)), ((), ())), preferred_element_type=jnp.float32)

    for k in range(1, nt):
        peer = lax.rem(mt + k, nt)
        slow[peer] = low_of(peer)
        pair_copy(slow, rlow, s_low, r_low, "tp", peer, mt).start()
    low = low_of(mt)
    for k in range(1, nt):
        peer = lax.rem(mt + k, nt)
        pair_copy(xe, full, s_xe, r_xe, "tp", peer, peer).wait_recv()
        pair_copy(slow, rlow, s_low, r_low, "tp", peer, peer).wait_recv()
        low = low + rlow[peer]
    low = low.T.astype(jnp.bfloat16)
    here = lax.broadcasted_iota(jnp.int32, (BLOCK, wide), 0) < live[mt]
    for c in range(CHUNKS):
        cols = slice(c * wide, (c + 1) * wide)
        up = full[:, :, cols].reshape(nt * ranks, wide)
        total = own[:, cols] + 0.5 * jnp.dot(low, up, preferred_element_type=jnp.float32)
        for k in range(1, nt):
            peer = lax.rem(mt + k, nt)
            base_copy(c, peer, peer).wait_recv()
            total = total + rb[c, peer].astype(jnp.float32)
        out[:, cols] = jnp.where(here, total, 0.0).astype(jnp.bfloat16)

    for k in range(1, nt):
        peer = lax.rem(mt + k, nt)
        for c in range(CHUNKS):
            base_copy(c, peer, mt).wait_send()
        pair_copy(xe, full, s_xe, r_xe, "tp", peer, mt).wait_send()
        pair_copy(slow, rlow, s_low, r_low, "tp", peer, mt).wait_send()
    for k in range(1, nm):
        g = lax.rem(mm + k, nm)
        pair_copy(sex, alle, s_ex, r_ex, "mem", g, mm, SLOTS).wait_send()
        pair_copy(ssh, allsh, s_sh, r_sh, "mem", g, mm, SLOTS).wait_send()


def body(
    activations,
    base_weight,
    pool_shrink,
    pool_expand,
    cache_shrink,
    cache_expand,
    adapter_home,
    evict_adapters,
    evict_slots,
    block_slot,
    block_live_rows,
):
    nm, nt = lax.axis_size("mem"), lax.axis_size("tp")
    rows, depth = activations.shape
    ranks = pool_expand.shape[1] // VALUE_FEATURES
    if rows != nt * BLOCK or ranks % 16 != 0:
        return plain_body(
            activations, base_weight, pool_shrink, pool_expand, cache_shrink, cache_expand,
            adapter_home, evict_adapters, evict_slots, block_slot, block_live_rows)
    pool_dev, rank = pool_shrink.shape[:2]
    wide = VALUE_FEATURES // CHUNKS
    bf, f32 = jnp.bfloat16, jnp.float32
    dma = pltpu.SemaphoreType.DMA
    any_spec = pl.BlockSpec(memory_space=pl.ANY)
    smem = pl.BlockSpec(memory_space=pltpu.SMEM)
    return pl.pallas_call(
        functools.partial(kernel, nm, nt),
        out_shape=jax.ShapeDtypeStruct((BLOCK, VALUE_FEATURES), bf),
        in_specs=[any_spec] * 6 + [smem] * 5,
        out_specs=pl.BlockSpec(memory_space=pltpu.VMEM),
        scratch_shapes=[
            pltpu.VMEM((rows, depth), bf),
            pltpu.VMEM((CHUNKS, depth, wide), bf),
            pltpu.VMEM((pool_dev, rank, depth), bf),
            pltpu.VMEM((ranks * pool_dev, VALUE_FEATURES), bf),
            pltpu.VMEM((SLOTS + nm, rank, depth), bf),
            pltpu.VMEM((SLOTS + nm, ranks, VALUE_FEATURES), bf),
            pltpu.VMEM((nm, rank, depth), bf),
            pltpu.VMEM((nm, ranks, VALUE_FEATURES), bf),
            pltpu.VMEM((nt, ranks, VALUE_FEATURES), bf),
            pltpu.VMEM((nt, ranks, VALUE_FEATURES), bf),
            pltpu.VMEM((rows, wide), f32),
            pltpu.VMEM((BLOCK, VALUE_FEATURES), f32),
            pltpu.VMEM((CHUNKS, nt, BLOCK, wide), bf),
            pltpu.VMEM((CHUNKS, nt, BLOCK, wide), bf),
            pltpu.VMEM((nt, rank, BLOCK), f32),
            pltpu.VMEM((nt, rank, BLOCK), f32),
            dma((8,)),
            dma((ranks,)),
            dma((CHUNKS, nt)), dma((CHUNKS, nt)),
            dma((nm,)), dma((nm,)),
            dma((nm,)), dma((nm,)),
            dma((nt,)), dma((nt,)),
            dma((nt,)), dma((nt,)),
        ],
        compiler_params=pltpu.CompilerParams(
            collective_id=0, has_side_effects=True, vmem_limit_bytes=48 * 1024 * 1024),
        cost_estimate=pl.CostEstimate(
            flops=2 * rows * depth * (VALUE_FEATURES + rank), bytes_accessed=16 * 1024 * 1024, transcendentals=0),
    )(
        activations, base_weight, pool_shrink, pool_expand, cache_shrink,
        cache_expand.reshape(SLOTS, ranks, VALUE_FEATURES),
        adapter_home, evict_adapters, evict_slots, block_slot, block_live_rows,
    )


def solution(mesh):
    placed = (
        P(("rep", "mem"), "tp"),
        P("tp", None),
        P("mem", None, "tp"),
        P("mem", "tp"),
        P(("rep", "mem"), None, "tp"),
        P(("rep", "mem"), "tp"),
        P("rep"),
        P("rep", None),
        P(("rep", "mem"), None),
        P(("rep", "mem")),
        P(("rep", "mem")),
    )
    return jax.shard_map(
        body, mesh=mesh, in_specs=placed, out_specs=P(("rep", "mem", "tp"), None), check_vma=False
    )
```

```python
import functools

import jax
import jax.numpy as jnp
from jax import lax
from jax.experimental import pallas as pl
from jax.experimental.pallas import tpu as pltpu
from jax.sharding import PartitionSpec as P

VALUE_FEATURES = 1024
BLOCK = 128
CAP = 1
SLOTS = 4
EVICT = 2


def plain_body(
    activations,
    base_weight,
    pool_shrink,
    pool_expand,
    cache_shrink,
    cache_expand,
    adapter_home,
    evict_adapters,
    evict_slots,
    block_slot,
    block_live_rows,
):
    groups = lax.axis_size("mem")
    tp_count = lax.axis_size("tp")
    group_index = lax.axis_index("mem")
    pool_dev = pool_shrink.shape[0]
    home = adapter_home[evict_adapters]
    owner = home // pool_dev
    position = jnp.arange(EVICT, dtype=jnp.int32)
    same = owner[:, :, None] == owner[:, None, :]
    earlier = position[None, None, :] < position[None, :, None]
    rank = jnp.sum((same & earlier).astype(jnp.int32), axis=2)
    local_row = home - owner * pool_dev
    wanted = (owner == group_index)[:, None, :] & (
        rank[:, None, :] == jnp.arange(CAP, dtype=jnp.int32)[None, :, None]
    )
    send_row = jnp.sum(jnp.where(wanted, local_row[:, None, :], 0), axis=2)
    got_shrink, got_expand = (
        lax.all_to_all(pool_shrink[send_row], "mem", split_axis=0, concat_axis=0, tiled=True),
        lax.all_to_all(pool_expand[send_row], "mem", split_axis=0, concat_axis=0, tiled=True),
    )
    my_owner = lax.dynamic_index_in_dim(owner, group_index, 0, keepdims=False)
    my_rank = lax.dynamic_index_in_dim(rank, group_index, 0, keepdims=False)
    flat = my_owner * CAP + my_rank
    new_shrink = got_shrink.reshape((groups * CAP,) + got_shrink.shape[2:])[flat]
    new_expand = got_expand.reshape(groups * CAP, got_expand.shape[2])[flat]
    targets = evict_slots[0]
    slot_shrink = cache_shrink.at[targets].set(new_shrink)
    slot_expand = cache_expand.at[targets].set(new_expand)
    rows = activations.shape[0]
    nblocks = rows // BLOCK
    blocked = activations.reshape(nblocks, BLOCK, activations.shape[1])
    lowrank_state = jnp.einsum(
        "nbd,nrd->nbr", blocked, slot_shrink[block_slot], preferred_element_type=jnp.float32
    ).reshape(rows, -1)
    row_ids = jnp.arange(rows, dtype=jnp.int32)
    block_hot = (row_ids // BLOCK)[:, None] == jnp.arange(nblocks, dtype=jnp.int32)[None, :]
    row_slot = jnp.sum(jnp.where(block_hot, block_slot[None, :], 0), axis=1)
    row_live = row_ids % BLOCK < jnp.sum(jnp.where(block_hot, block_live_rows[None, :], 0), axis=1)
    slot_hot = row_slot[:, None] == jnp.arange(SLOTS, dtype=jnp.int32)[None, :]
    own = rows // tp_count
    start = lax.axis_index("tp") * own
    zero_value = jnp.zeros((), jnp.bfloat16)
    base_rows = lax.psum_scatter(
        jnp.dot(activations, base_weight, preferred_element_type=jnp.float32),
        "tp",
        scatter_dimension=0,
        tiled=True,
    )
    low_rows = lax.psum_scatter(lowrank_state, "tp", scatter_dimension=0, tiled=True).astype(
        jnp.bfloat16
    )
    full_expand = lax.all_gather(slot_expand, "tp", axis=1, tiled=True).reshape(-1, VALUE_FEATURES)
    own_hot = lax.dynamic_slice_in_dim(slot_hot, start, own, 0)
    chosen = jnp.where(own_hot[:, :, None], low_rows[:, None, :], zero_value).reshape(own, -1)
    total = base_rows + 0.5 * jnp.dot(chosen, full_expand, preferred_element_type=jnp.float32)
    own_live = lax.dynamic_slice_in_dim(row_live, start, own, 0)
    return jnp.where(own_live[:, None], total, 0.0).astype(jnp.bfloat16)


CHUNKS = 4
MESH = pl.DeviceIdType.MESH


def kernel(
    nm, nt, act_h, w_h, psh_h, pex_h, csh_h, cex_h, home_h, evict_h, eslot_h, bslot_h, live_h,
    out,
    home, evict, eslot, bslot, live, cx, hold, relay,
    act, w, psh, pst, allsh, alle, ssh, sex, xe, full, pf, own, sb, rb, slow, rlow,
    loc, int_sem, pex_sem, s_rel, r_rel, s_base, r_base, s_sh, r_sh, s_ex, r_ex, s_xe, r_xe, s_low, r_low,
):
    mm = lax.axis_index("mem")
    mt = lax.axis_index("tp")
    pool_dev = psh_h.shape[0]
    ranks = cex_h.shape[1] // VALUE_FEATURES
    near = mt + 1 - 2 * lax.rem(mt, 2)
    other = lax.rem(mt + 2, nt)
    far = nt - 1 - mt
    edge = (mt == 0) | (mt == nt - 1)
    inner = (mt > 0) & (mt < nt - 1)
    wide = w_h.shape[1] // CHUNKS

    barrier = pltpu.get_barrier_semaphore()
    for k in range(1, nt):
        pl.semaphore_signal(barrier, inc=1, device_id={"tp": lax.rem(mt + k, nt)}, device_id_type=MESH)
    for k in range(1, nm):
        pl.semaphore_signal(barrier, inc=1, device_id={"mem": lax.rem(mm + k, nm)}, device_id_type=MESH)

    load_int = []
    for n, (a, b) in enumerate(((home_h, home), (evict_h, evict), (eslot_h, eslot), (bslot_h, bslot), (live_h, live))):
        load_int.append(pltpu.make_async_copy(a, b, int_sem.at[n]))
    load_act = pltpu.make_async_copy(act_h, act, loc.at[0])
    load_act.start()
    load_w = []
    for c in range(CHUNKS):
        load_w.append(pltpu.make_async_copy(w_h.at[:, pl.ds(c * wide, wide)], w.at[c], loc.at[1 + c]))
        load_w[c].start()
    for copy in load_int:
        copy.start()
    load_pex = []
    for r in range(ranks):
        load_pex.append(pltpu.make_async_copy(
            pex_h.at[:, pl.ds(r * VALUE_FEATURES, VALUE_FEATURES)],
            pst.at[pl.ds(r * pool_dev, pool_dev), :],
            pex_sem.at[r],
        ))
        load_pex[r].start()
    load_psh = pltpu.make_async_copy(psh_h, psh, loc.at[5])
    load_psh.start()
    load_csh = pltpu.make_async_copy(csh_h, allsh.at[pl.ds(0, SLOTS)], loc.at[6])
    load_csh.start()
    load_cex = pltpu.make_async_copy(cex_h, cx, loc.at[7])
    load_cex.start()

    def base_copy(c, peer, slot):
        return pltpu.make_async_remote_copy(
            src_ref=sb.at[c, peer], dst_ref=rb.at[c, slot],
            send_sem=s_base.at[c, peer], recv_sem=r_base.at[c, slot],
            device_id={"tp": peer}, device_id_type=MESH)

    def relay_copy(c):
        return pltpu.make_async_remote_copy(
            src_ref=sb.at[c, far], dst_ref=relay.at[c], send_sem=s_rel.at[c], recv_sem=r_rel.at[c],
            device_id={"tp": near}, device_id_type=MESH)

    def pair_copy(a, b, ss, rs, axis, peer, slot, base=0):
        return pltpu.make_async_remote_copy(
            src_ref=a.at[peer], dst_ref=b.at[base + slot],
            send_sem=ss.at[peer], recv_sem=rs.at[slot],
            device_id={axis: peer}, device_id_type=MESH)

    load_act.wait()
    for c in range(CHUNKS):
        load_w[c].wait()
        pf[...] = jnp.dot(act[...], w[c], preferred_element_type=jnp.float32)
        if c == 0:
            pl.semaphore_wait(barrier, nt - 1 + nm - 1)

        def part(b):
            return pf[pl.ds(pl.multiple_of(b * BLOCK, BLOCK), BLOCK), :]

        sb[c, far] = part(far).astype(jnp.bfloat16)

        @pl.when(edge)
        def _():
            relay_copy(c).start()
            sb[c, other] = part(other).astype(jnp.bfloat16)
            base_copy(c, other, mt).start()

        @pl.when(inner)
        def _():
            base_copy(c, far, mt).start()
            hold[c] = part(other)

        sb[c, near] = part(near).astype(jnp.bfloat16)

        @pl.when(inner)
        def _():
            base_copy(c, near, mt).start()

        own[:, c * wide:(c + 1) * wide] = part(mt)

    @pl.when(edge)
    def _():
        for c in range(CHUNKS):
            base_copy(c, near, mt).start()

    for copy in load_int:
        copy.wait()

    def wanted(g):
        row = jnp.int32(0)
        for e in range(EVICT):
            h = home[evict[e, g]]
            o = lax.div(h, jnp.int32(pool_dev))
            row = jnp.where(o == mm, h - o * pool_dev, row)
        return row

    rows = [wanted(g) for g in range(nm)]
    shape = (nm * ranks, ranks * pool_dev)
    i = lax.broadcasted_iota(jnp.int32, shape, 0)
    q = lax.broadcasted_iota(jnp.int32, shape, 1)
    target = jnp.zeros(shape, jnp.int32)
    for g in range(nm):
        target = jnp.where((i >= g * ranks) & (i < (g + 1) * ranks), (i - g * ranks) * pool_dev + rows[g], target)
    hot = jnp.where(q == target, 1.0, 0.0).astype(jnp.bfloat16)
    for r in range(ranks):
        load_pex[r].wait()
    picked = jnp.dot(hot, pst[...], preferred_element_type=jnp.float32).astype(jnp.bfloat16)
    sex[...] = picked.reshape(nm, ranks, VALUE_FEATURES)
    for k in range(1, nm):
        pair_copy(sex, alle, s_ex, r_ex, "mem", lax.rem(mm + k, nm), mm, SLOTS).start()
    alle[SLOTS + mm] = sex[mm]
    load_psh.wait()
    for k in range(1, nm):
        g = lax.rem(mm + k, nm)
        ssh[g] = psh[wanted(g)]
        pair_copy(ssh, allsh, s_sh, r_sh, "mem", g, mm, SLOTS).start()
    allsh[SLOTS + mm] = psh[wanted(mm)]

    owner = [lax.div(home[evict[e, mm]], jnp.int32(pool_dev)) for e in range(EVICT)]

    def place(b):
        c = bslot[b]
        index = c
        for e in range(EVICT):
            index = jnp.where(eslot[0, e] == c, SLOTS + owner[e], index)
        return index

    @pl.when(inner)
    def _():
        for c in range(CHUNKS):
            relay_copy(c).wait_recv()
            sb[c, other] = (hold[c] + relay[c].astype(jnp.float32)).astype(jnp.bfloat16)
            base_copy(c, other, mt).start()

    load_cex.wait()
    shape = (SLOTS * ranks, SLOTS)
    i = lax.broadcasted_iota(jnp.int32, shape, 0)
    q = lax.broadcasted_iota(jnp.int32, shape, 1)
    kept = jnp.zeros((SLOTS * ranks, VALUE_FEATURES), jnp.float32)
    for r in range(ranks):
        hot = jnp.where(i == q * ranks + r, 1.0, 0.0).astype(jnp.bfloat16)
        kept += jnp.dot(
            hot, cx[:, r * VALUE_FEATURES:(r + 1) * VALUE_FEATURES], preferred_element_type=jnp.float32)
    alle[0:SLOTS] = kept.astype(jnp.bfloat16).reshape(SLOTS, ranks, VALUE_FEATURES)
    for k in range(1, nm):
        pair_copy(sex, alle, s_ex, r_ex, "mem", lax.rem(mm + k, nm), lax.rem(mm + k, nm), SLOTS).wait_recv()
    for k in range(1, nt):
        peer = lax.rem(mt + k, nt)
        xe[peer] = alle[place(peer)]
        pair_copy(xe, full, s_xe, r_xe, "tp", peer, mt).start()
    full[mt] = alle[place(mt)]

    load_csh.wait()
    for k in range(1, nm):
        pair_copy(ssh, allsh, s_sh, r_sh, "mem", lax.rem(mm + k, nm), lax.rem(mm + k, nm), SLOTS).wait_recv()

    def low_of(b):
        return lax.dot_general(
            allsh[place(b)], act[pl.ds(pl.multiple_of(b * BLOCK, BLOCK), BLOCK), :],
            (((1,), (1,)), ((), ())), preferred_element_type=jnp.float32)

    for k in range(1, nt):
        peer = lax.rem(mt + k, nt)
        slow[peer] = low_of(peer)
        pair_copy(slow, rlow, s_low, r_low, "tp", peer, mt).start()
    low = low_of(mt)
    for k in range(1, nt):
        peer = lax.rem(mt + k, nt)
        pair_copy(xe, full, s_xe, r_xe, "tp", peer, peer).wait_recv()
        pair_copy(slow, rlow, s_low, r_low, "tp", peer, peer).wait_recv()
        low = low + rlow[peer]
    low = low.T.astype(jnp.bfloat16)
    here = lax.broadcasted_iota(jnp.int32, (BLOCK, wide), 0) < live[mt]

    @pl.when(inner)
    def _():
        for c in range(CHUNKS):
            base_copy(c, far, far).wait_recv()
            own[:, c * wide:(c + 1) * wide] += rb[c, far].astype(jnp.float32)

    for c in range(CHUNKS):
        cols = slice(c * wide, (c + 1) * wide)
        up = full[:, :, cols].reshape(nt * ranks, wide)
        total = own[:, cols] + 0.5 * jnp.dot(low, up, preferred_element_type=jnp.float32)
        for peer in (near, other):
            base_copy(c, peer, peer).wait_recv()
            total = total + rb[c, peer].astype(jnp.float32)
        out[:, cols] = jnp.where(here, total, 0.0).astype(jnp.bfloat16)

    for c in range(CHUNKS):
        base_copy(c, near, mt).wait_send()
        base_copy(c, other, mt).wait_send()

        @pl.when(edge)
        def _():
            relay_copy(c).wait_send()

        @pl.when(inner)
        def _():
            base_copy(c, far, mt).wait_send()

    for k in range(1, nt):
        peer = lax.rem(mt + k, nt)
        pair_copy(xe, full, s_xe, r_xe, "tp", peer, mt).wait_send()
        pair_copy(slow, rlow, s_low, r_low, "tp", peer, mt).wait_send()
    for k in range(1, nm):
        g = lax.rem(mm + k, nm)
        pair_copy(sex, alle, s_ex, r_ex, "mem", g, mm, SLOTS).wait_send()
        pair_copy(ssh, allsh, s_sh, r_sh, "mem", g, mm, SLOTS).wait_send()


def body(
    activations,
    base_weight,
    pool_shrink,
    pool_expand,
    cache_shrink,
    cache_expand,
    adapter_home,
    evict_adapters,
    evict_slots,
    block_slot,
    block_live_rows,
):
    nm, nt = lax.axis_size("mem"), lax.axis_size("tp")
    rows, depth = activations.shape
    ranks = pool_expand.shape[1] // VALUE_FEATURES
    if nt != 4 or rows != nt * BLOCK or ranks % 16 != 0:
        return plain_body(
            activations, base_weight, pool_shrink, pool_expand, cache_shrink, cache_expand,
            adapter_home, evict_adapters, evict_slots, block_slot, block_live_rows)
    pool_dev, rank = pool_shrink.shape[:2]
    wide = VALUE_FEATURES // CHUNKS
    bf, f32 = jnp.bfloat16, jnp.float32
    dma = pltpu.SemaphoreType.DMA
    any_spec = pl.BlockSpec(memory_space=pl.ANY)
    return pl.pallas_call(
        functools.partial(kernel, nm, nt),
        out_shape=jax.ShapeDtypeStruct((BLOCK, VALUE_FEATURES), bf),
        in_specs=[any_spec] * 11,
        out_specs=pl.BlockSpec(memory_space=pltpu.VMEM),
        scratch_shapes=[
            pltpu.SMEM(adapter_home.shape, jnp.int32),
            pltpu.SMEM(evict_adapters.shape[::-1], jnp.int32),
            pltpu.SMEM(evict_slots.shape, jnp.int32),
            pltpu.SMEM(block_slot.shape, jnp.int32),
            pltpu.SMEM(block_live_rows.shape, jnp.int32),
            pltpu.VMEM(cache_expand.shape, bf),
            pltpu.VMEM((CHUNKS, BLOCK, wide), f32),
            pltpu.VMEM((CHUNKS, BLOCK, wide), bf),
            pltpu.VMEM((rows, depth), bf),
            pltpu.VMEM((CHUNKS, depth, wide), bf),
            pltpu.VMEM((pool_dev, rank, depth), bf),
            pltpu.VMEM((ranks * pool_dev, VALUE_FEATURES), bf),
            pltpu.VMEM((SLOTS + nm, rank, depth), bf),
            pltpu.VMEM((SLOTS + nm, ranks, VALUE_FEATURES), bf),
            pltpu.VMEM((nm, rank, depth), bf),
            pltpu.VMEM((nm, ranks, VALUE_FEATURES), bf),
            pltpu.VMEM((nt, ranks, VALUE_FEATURES), bf),
            pltpu.VMEM((nt, ranks, VALUE_FEATURES), bf),
            pltpu.VMEM((rows, wide), f32),
            pltpu.VMEM((BLOCK, VALUE_FEATURES), f32),
            pltpu.VMEM((CHUNKS, nt, BLOCK, wide), bf),
            pltpu.VMEM((CHUNKS, nt, BLOCK, wide), bf),
            pltpu.VMEM((nt, rank, BLOCK), f32),
            pltpu.VMEM((nt, rank, BLOCK), f32),
            dma((8,)),
            dma((5,)),
            dma((ranks,)),
            dma((CHUNKS,)), dma((CHUNKS,)),
            dma((CHUNKS, nt)), dma((CHUNKS, nt)),
            dma((nm,)), dma((nm,)),
            dma((nm,)), dma((nm,)),
            dma((nt,)), dma((nt,)),
            dma((nt,)), dma((nt,)),
        ],
        compiler_params=pltpu.CompilerParams(
            collective_id=0, has_side_effects=True, vmem_limit_bytes=60 * 1024 * 1024),
        cost_estimate=pl.CostEstimate(
            flops=2 * rows * depth * (VALUE_FEATURES + rank), bytes_accessed=16 * 1024 * 1024, transcendentals=0),
    )(
        activations, base_weight, pool_shrink, pool_expand, cache_shrink,
        cache_expand,
        adapter_home, evict_adapters.T, evict_slots, block_slot, block_live_rows,
    )


def solution(mesh):
    placed = (
        P(("rep", "mem"), "tp"),
        P("tp", None),
        P("mem", None, "tp"),
        P("mem", "tp"),
        P(("rep", "mem"), None, "tp"),
        P(("rep", "mem"), "tp"),
        P("rep"),
        P("rep", None),
        P(("rep", "mem"), None),
        P(("rep", "mem")),
        P(("rep", "mem")),
    )
    return jax.shard_map(
        body, mesh=mesh, in_specs=placed, out_specs=P(("rep", "mem", "tp"), None), check_vma=False
    )
```

```python
import functools

import jax
import jax.numpy as jnp
from jax import lax
from jax.experimental import pallas as pl
from jax.experimental.pallas import tpu as pltpu
from jax.sharding import PartitionSpec as P

VALUE_FEATURES = 1024
BLOCK = 128
CAP = 1
SLOTS = 4
EVICT = 2


def plain_body(
    activations,
    base_weight,
    pool_shrink,
    pool_expand,
    cache_shrink,
    cache_expand,
    adapter_home,
    evict_adapters,
    evict_slots,
    block_slot,
    block_live_rows,
):
    groups = lax.axis_size("mem")
    tp_count = lax.axis_size("tp")
    group_index = lax.axis_index("mem")
    pool_dev = pool_shrink.shape[0]
    home = adapter_home[evict_adapters]
    owner = home // pool_dev
    position = jnp.arange(EVICT, dtype=jnp.int32)
    same = owner[:, :, None] == owner[:, None, :]
    earlier = position[None, None, :] < position[None, :, None]
    rank = jnp.sum((same & earlier).astype(jnp.int32), axis=2)
    local_row = home - owner * pool_dev
    wanted = (owner == group_index)[:, None, :] & (
        rank[:, None, :] == jnp.arange(CAP, dtype=jnp.int32)[None, :, None]
    )
    send_row = jnp.sum(jnp.where(wanted, local_row[:, None, :], 0), axis=2)
    got_shrink, got_expand = (
        lax.all_to_all(pool_shrink[send_row], "mem", split_axis=0, concat_axis=0, tiled=True),
        lax.all_to_all(pool_expand[send_row], "mem", split_axis=0, concat_axis=0, tiled=True),
    )
    my_owner = lax.dynamic_index_in_dim(owner, group_index, 0, keepdims=False)
    my_rank = lax.dynamic_index_in_dim(rank, group_index, 0, keepdims=False)
    flat = my_owner * CAP + my_rank
    new_shrink = got_shrink.reshape((groups * CAP,) + got_shrink.shape[2:])[flat]
    new_expand = got_expand.reshape(groups * CAP, got_expand.shape[2])[flat]
    targets = evict_slots[0]
    slot_shrink = cache_shrink.at[targets].set(new_shrink)
    slot_expand = cache_expand.at[targets].set(new_expand)
    rows = activations.shape[0]
    nblocks = rows // BLOCK
    blocked = activations.reshape(nblocks, BLOCK, activations.shape[1])
    lowrank_state = jnp.einsum(
        "nbd,nrd->nbr", blocked, slot_shrink[block_slot], preferred_element_type=jnp.float32
    ).reshape(rows, -1)
    row_ids = jnp.arange(rows, dtype=jnp.int32)
    block_hot = (row_ids // BLOCK)[:, None] == jnp.arange(nblocks, dtype=jnp.int32)[None, :]
    row_slot = jnp.sum(jnp.where(block_hot, block_slot[None, :], 0), axis=1)
    row_live = row_ids % BLOCK < jnp.sum(jnp.where(block_hot, block_live_rows[None, :], 0), axis=1)
    slot_hot = row_slot[:, None] == jnp.arange(SLOTS, dtype=jnp.int32)[None, :]
    own = rows // tp_count
    start = lax.axis_index("tp") * own
    zero_value = jnp.zeros((), jnp.bfloat16)
    base_rows = lax.psum_scatter(
        jnp.dot(activations, base_weight, preferred_element_type=jnp.float32),
        "tp",
        scatter_dimension=0,
        tiled=True,
    )
    low_rows = lax.psum_scatter(lowrank_state, "tp", scatter_dimension=0, tiled=True).astype(
        jnp.bfloat16
    )
    full_expand = lax.all_gather(slot_expand, "tp", axis=1, tiled=True).reshape(-1, VALUE_FEATURES)
    own_hot = lax.dynamic_slice_in_dim(slot_hot, start, own, 0)
    chosen = jnp.where(own_hot[:, :, None], low_rows[:, None, :], zero_value).reshape(own, -1)
    total = base_rows + 0.5 * jnp.dot(chosen, full_expand, preferred_element_type=jnp.float32)
    own_live = lax.dynamic_slice_in_dim(row_live, start, own, 0)
    return jnp.where(own_live[:, None], total, 0.0).astype(jnp.bfloat16)


CHUNKS = 4
MESH = pl.DeviceIdType.MESH


def kernel(
    nm, nt, act_h, w_h, psh_h, pex_h, csh_h, cex_h, home_h, evict_h, eslot_h, bslot_h, live_h,
    out,
    home, evict, eslot, bslot, live, cx, hold, relay,
    act, w, psh, pst, allsh, alle, ssh, sex, xe, full, pf, own, sb, rb, slow, rlow,
    loc, int_sem, pex_sem, s_rel, r_rel, s_base, r_base, s_sh, r_sh, s_ex, r_ex, s_xe, r_xe, s_low, r_low,
):
    mm = lax.axis_index("mem")
    mt = lax.axis_index("tp")
    pool_dev = psh_h.shape[0]
    ranks = cex_h.shape[1] // VALUE_FEATURES
    near = mt + 1 - 2 * lax.rem(mt, 2)
    other = lax.rem(mt + 2, nt)
    far = nt - 1 - mt
    edge = (mt == 0) | (mt == nt - 1)
    inner = (mt > 0) & (mt < nt - 1)
    wide = w_h.shape[1] // CHUNKS

    barrier = pltpu.get_barrier_semaphore()
    for k in range(1, nt):
        pl.semaphore_signal(barrier, inc=1, device_id={"tp": lax.rem(mt + k, nt)}, device_id_type=MESH)
    for k in range(1, nm):
        pl.semaphore_signal(barrier, inc=1, device_id={"mem": lax.rem(mm + k, nm)}, device_id_type=MESH)

    load_int = []
    for n, (a, b) in enumerate(((home_h, home), (evict_h, evict), (eslot_h, eslot), (bslot_h, bslot), (live_h, live))):
        load_int.append(pltpu.make_async_copy(a, b, int_sem.at[n]))
    load_act = pltpu.make_async_copy(act_h, act, loc.at[0])
    load_act.start()
    load_w = []
    for c in range(CHUNKS):
        load_w.append(pltpu.make_async_copy(w_h.at[:, pl.ds(c * wide, wide)], w.at[c], loc.at[1 + c]))
    load_w[0].start()
    load_w[1].start()
    load_pex = []
    for r in range(ranks):
        load_pex.append(pltpu.make_async_copy(
            pex_h.at[:, pl.ds(r * VALUE_FEATURES, VALUE_FEATURES)],
            pst.at[pl.ds(r * pool_dev, pool_dev), :],
            pex_sem.at[r],
        ))
    load_psh = pltpu.make_async_copy(psh_h, psh, loc.at[5])
    load_csh = pltpu.make_async_copy(csh_h, allsh.at[pl.ds(0, SLOTS)], loc.at[6])
    load_cex = pltpu.make_async_copy(cex_h, cx, loc.at[7])

    def base_copy(c, peer, slot):
        return pltpu.make_async_remote_copy(
            src_ref=sb.at[c, peer], dst_ref=rb.at[c, slot],
            send_sem=s_base.at[c, peer], recv_sem=r_base.at[c, slot],
            device_id={"tp": peer}, device_id_type=MESH)

    def relay_copy(c):
        return pltpu.make_async_remote_copy(
            src_ref=sb.at[c, far], dst_ref=relay.at[c], send_sem=s_rel.at[c], recv_sem=r_rel.at[c],
            device_id={"tp": near}, device_id_type=MESH)

    def pair_copy(a, b, ss, rs, axis, peer, slot, base=0):
        return pltpu.make_async_remote_copy(
            src_ref=a.at[peer], dst_ref=b.at[base + slot],
            send_sem=ss.at[peer], recv_sem=rs.at[slot],
            device_id={axis: peer}, device_id_type=MESH)

    load_act.wait()
    for c in range(CHUNKS):
        load_w[c].wait()
        if c == 0:
            load_w[2].start()
            load_w[3].start()
            for copy in load_int + load_pex:
                copy.start()
        if c == 2:
            load_psh.start()
            load_csh.start()
            load_cex.start()
        pf[...] = jnp.dot(act[...], w[c], preferred_element_type=jnp.float32)
        if c == 0:
            pl.semaphore_wait(barrier, nt - 1 + nm - 1)

        def part(b):
            return pf[pl.ds(pl.multiple_of(b * BLOCK, BLOCK), BLOCK), :]

        sb[c, far] = part(far).astype(jnp.bfloat16)

        @pl.when(edge)
        def _():
            relay_copy(c).start()
            sb[c, other] = part(other).astype(jnp.bfloat16)
            base_copy(c, other, mt).start()

        @pl.when(inner)
        def _():
            base_copy(c, far, mt).start()
            hold[c] = part(other)

        sb[c, near] = part(near).astype(jnp.bfloat16)

        @pl.when(inner)
        def _():
            base_copy(c, near, mt).start()

        own[:, c * wide:(c + 1) * wide] = part(mt)

    @pl.when(edge)
    def _():
        for c in range(CHUNKS):
            base_copy(c, near, mt).start()

    for copy in load_int:
        copy.wait()

    def wanted(g):
        row = jnp.int32(0)
        for e in range(EVICT):
            h = home[evict[e, g]]
            o = lax.div(h, jnp.int32(pool_dev))
            row = jnp.where(o == mm, h - o * pool_dev, row)
        return row

    rows = [wanted(g) for g in range(nm)]
    shape = (nm * ranks, ranks * pool_dev)
    i = lax.broadcasted_iota(jnp.int32, shape, 0)
    q = lax.broadcasted_iota(jnp.int32, shape, 1)
    target = jnp.zeros(shape, jnp.int32)
    for g in range(nm):
        target = jnp.where((i >= g * ranks) & (i < (g + 1) * ranks), (i - g * ranks) * pool_dev + rows[g], target)
    hot = jnp.where(q == target, 1.0, 0.0).astype(jnp.bfloat16)
    for r in range(ranks):
        load_pex[r].wait()
    picked = jnp.dot(hot, pst[...], preferred_element_type=jnp.float32).astype(jnp.bfloat16)
    sex[...] = picked.reshape(nm, ranks, VALUE_FEATURES)
    for k in range(1, nm):
        pair_copy(sex, alle, s_ex, r_ex, "mem", lax.rem(mm + k, nm), mm, SLOTS).start()
    alle[SLOTS + mm] = sex[mm]
    load_psh.wait()
    for k in range(1, nm):
        g = lax.rem(mm + k, nm)
        ssh[g] = psh[wanted(g)]
        pair_copy(ssh, allsh, s_sh, r_sh, "mem", g, mm, SLOTS).start()
    allsh[SLOTS + mm] = psh[wanted(mm)]

    owner = [lax.div(home[evict[e, mm]], jnp.int32(pool_dev)) for e in range(EVICT)]

    def place(b):
        c = bslot[b]
        index = c
        for e in range(EVICT):
            index = jnp.where(eslot[0, e] == c, SLOTS + owner[e], index)
        return index

    @pl.when(inner)
    def _():
        for c in range(CHUNKS):
            relay_copy(c).wait_recv()
            sb[c, other] = (hold[c] + relay[c].astype(jnp.float32)).astype(jnp.bfloat16)
            base_copy(c, other, mt).start()

    load_cex.wait()
    shape = (SLOTS * ranks, SLOTS)
    i = lax.broadcasted_iota(jnp.int32, shape, 0)
    q = lax.broadcasted_iota(jnp.int32, shape, 1)
    kept = jnp.zeros((SLOTS * ranks, VALUE_FEATURES), jnp.float32)
    for r in range(ranks):
        hot = jnp.where(i == q * ranks + r, 1.0, 0.0).astype(jnp.bfloat16)
        kept += jnp.dot(
            hot, cx[:, r * VALUE_FEATURES:(r + 1) * VALUE_FEATURES], preferred_element_type=jnp.float32)
    alle[0:SLOTS] = kept.astype(jnp.bfloat16).reshape(SLOTS, ranks, VALUE_FEATURES)
    for k in range(1, nm):
        pair_copy(sex, alle, s_ex, r_ex, "mem", lax.rem(mm + k, nm), lax.rem(mm + k, nm), SLOTS).wait_recv()
    for k in range(1, nt):
        peer = lax.rem(mt + k, nt)
        xe[peer] = alle[place(peer)]
        pair_copy(xe, full, s_xe, r_xe, "tp", peer, mt).start()
    full[mt] = alle[place(mt)]

    load_csh.wait()
    for k in range(1, nm):
        pair_copy(ssh, allsh, s_sh, r_sh, "mem", lax.rem(mm + k, nm), lax.rem(mm + k, nm), SLOTS).wait_recv()

    def low_of(b):
        return lax.dot_general(
            allsh[place(b)], act[pl.ds(pl.multiple_of(b * BLOCK, BLOCK), BLOCK), :],
            (((1,), (1,)), ((), ())), preferred_element_type=jnp.float32)

    for k in range(1, nt):
        peer = lax.rem(mt + k, nt)
        slow[peer] = low_of(peer)
        pair_copy(slow, rlow, s_low, r_low, "tp", peer, mt).start()
    low = low_of(mt)
    for k in range(1, nt):
        peer = lax.rem(mt + k, nt)
        pair_copy(xe, full, s_xe, r_xe, "tp", peer, peer).wait_recv()
        pair_copy(slow, rlow, s_low, r_low, "tp", peer, peer).wait_recv()
        low = low + rlow[peer]
    low = low.T.astype(jnp.bfloat16)
    here = lax.broadcasted_iota(jnp.int32, (BLOCK, wide), 0) < live[mt]

    @pl.when(inner)
    def _():
        for c in range(CHUNKS):
            base_copy(c, far, far).wait_recv()
            own[:, c * wide:(c + 1) * wide] += rb[c, far].astype(jnp.float32)

    for c in range(CHUNKS):
        cols = slice(c * wide, (c + 1) * wide)
        up = full[:, :, cols].reshape(nt * ranks, wide)
        total = own[:, cols] + 0.5 * jnp.dot(low, up, preferred_element_type=jnp.float32)
        for peer in (near, other):
            base_copy(c, peer, peer).wait_recv()
            total = total + rb[c, peer].astype(jnp.float32)
        out[:, cols] = jnp.where(here, total, 0.0).astype(jnp.bfloat16)

    for c in range(CHUNKS):
        base_copy(c, near, mt).wait_send()
        base_copy(c, other, mt).wait_send()

        @pl.when(edge)
        def _():
            relay_copy(c).wait_send()

        @pl.when(inner)
        def _():
            base_copy(c, far, mt).wait_send()

    for k in range(1, nt):
        peer = lax.rem(mt + k, nt)
        pair_copy(xe, full, s_xe, r_xe, "tp", peer, mt).wait_send()
        pair_copy(slow, rlow, s_low, r_low, "tp", peer, mt).wait_send()
    for k in range(1, nm):
        g = lax.rem(mm + k, nm)
        pair_copy(sex, alle, s_ex, r_ex, "mem", g, mm, SLOTS).wait_send()
        pair_copy(ssh, allsh, s_sh, r_sh, "mem", g, mm, SLOTS).wait_send()


def body(
    activations,
    base_weight,
    pool_shrink,
    pool_expand,
    cache_shrink,
    cache_expand,
    adapter_home,
    evict_adapters,
    evict_slots,
    block_slot,
    block_live_rows,
):
    nm, nt = lax.axis_size("mem"), lax.axis_size("tp")
    rows, depth = activations.shape
    ranks = pool_expand.shape[1] // VALUE_FEATURES
    if nt != 4 or rows != nt * BLOCK or ranks % 16 != 0:
        return plain_body(
            activations, base_weight, pool_shrink, pool_expand, cache_shrink, cache_expand,
            adapter_home, evict_adapters, evict_slots, block_slot, block_live_rows)
    pool_dev, rank = pool_shrink.shape[:2]
    wide = VALUE_FEATURES // CHUNKS
    bf, f32 = jnp.bfloat16, jnp.float32
    dma = pltpu.SemaphoreType.DMA
    any_spec = pl.BlockSpec(memory_space=pl.ANY)
    return pl.pallas_call(
        functools.partial(kernel, nm, nt),
        out_shape=jax.ShapeDtypeStruct((BLOCK, VALUE_FEATURES), bf),
        in_specs=[any_spec] * 11,
        out_specs=pl.BlockSpec(memory_space=pltpu.VMEM),
        scratch_shapes=[
            pltpu.SMEM(adapter_home.shape, jnp.int32),
            pltpu.SMEM(evict_adapters.shape[::-1], jnp.int32),
            pltpu.SMEM(evict_slots.shape, jnp.int32),
            pltpu.SMEM(block_slot.shape, jnp.int32),
            pltpu.SMEM(block_live_rows.shape, jnp.int32),
            pltpu.VMEM(cache_expand.shape, bf),
            pltpu.VMEM((CHUNKS, BLOCK, wide), f32),
            pltpu.VMEM((CHUNKS, BLOCK, wide), bf),
            pltpu.VMEM((rows, depth), bf),
            pltpu.VMEM((CHUNKS, depth, wide), bf),
            pltpu.VMEM((pool_dev, rank, depth), bf),
            pltpu.VMEM((ranks * pool_dev, VALUE_FEATURES), bf),
            pltpu.VMEM((SLOTS + nm, rank, depth), bf),
            pltpu.VMEM((SLOTS + nm, ranks, VALUE_FEATURES), bf),
            pltpu.VMEM((nm, rank, depth), bf),
            pltpu.VMEM((nm, ranks, VALUE_FEATURES), bf),
            pltpu.VMEM((nt, ranks, VALUE_FEATURES), bf),
            pltpu.VMEM((nt, ranks, VALUE_FEATURES), bf),
            pltpu.VMEM((rows, wide), f32),
            pltpu.VMEM((BLOCK, VALUE_FEATURES), f32),
            pltpu.VMEM((CHUNKS, nt, BLOCK, wide), bf),
            pltpu.VMEM((CHUNKS, nt, BLOCK, wide), bf),
            pltpu.VMEM((nt, rank, BLOCK), f32),
            pltpu.VMEM((nt, rank, BLOCK), f32),
            dma((8,)),
            dma((5,)),
            dma((ranks,)),
            dma((CHUNKS,)), dma((CHUNKS,)),
            dma((CHUNKS, nt)), dma((CHUNKS, nt)),
            dma((nm,)), dma((nm,)),
            dma((nm,)), dma((nm,)),
            dma((nt,)), dma((nt,)),
            dma((nt,)), dma((nt,)),
        ],
        compiler_params=pltpu.CompilerParams(
            collective_id=0, has_side_effects=True, vmem_limit_bytes=60 * 1024 * 1024),
        cost_estimate=pl.CostEstimate(
            flops=2 * rows * depth * (VALUE_FEATURES + rank), bytes_accessed=16 * 1024 * 1024, transcendentals=0),
    )(
        activations, base_weight, pool_shrink, pool_expand, cache_shrink,
        cache_expand,
        adapter_home, evict_adapters.T, evict_slots, block_slot, block_live_rows,
    )


def solution(mesh):
    placed = (
        P(("rep", "mem"), "tp"),
        P("tp", None),
        P("mem", None, "tp"),
        P("mem", "tp"),
        P(("rep", "mem"), None, "tp"),
        P(("rep", "mem"), "tp"),
        P("rep"),
        P("rep", None),
        P(("rep", "mem"), None),
        P(("rep", "mem")),
        P(("rep", "mem")),
    )
    return jax.shard_map(
        body, mesh=mesh, in_specs=placed, out_specs=P(("rep", "mem", "tp"), None), check_vma=False
    )
```

```python
import functools

import jax
import jax.numpy as jnp
from jax import lax
from jax.experimental import pallas as pl
from jax.experimental.pallas import tpu as pltpu
from jax.sharding import PartitionSpec as P

VALUE_FEATURES = 1024
BLOCK = 128
CAP = 1
SLOTS = 4
EVICT = 2


def plain_body(
    activations,
    base_weight,
    pool_shrink,
    pool_expand,
    cache_shrink,
    cache_expand,
    adapter_home,
    evict_adapters,
    evict_slots,
    block_slot,
    block_live_rows,
):
    groups = lax.axis_size("mem")
    tp_count = lax.axis_size("tp")
    group_index = lax.axis_index("mem")
    pool_dev = pool_shrink.shape[0]
    home = adapter_home[evict_adapters]
    owner = home // pool_dev
    position = jnp.arange(EVICT, dtype=jnp.int32)
    same = owner[:, :, None] == owner[:, None, :]
    earlier = position[None, None, :] < position[None, :, None]
    rank = jnp.sum((same & earlier).astype(jnp.int32), axis=2)
    local_row = home - owner * pool_dev
    wanted = (owner == group_index)[:, None, :] & (
        rank[:, None, :] == jnp.arange(CAP, dtype=jnp.int32)[None, :, None]
    )
    send_row = jnp.sum(jnp.where(wanted, local_row[:, None, :], 0), axis=2)
    got_shrink, got_expand = (
        lax.all_to_all(pool_shrink[send_row], "mem", split_axis=0, concat_axis=0, tiled=True),
        lax.all_to_all(pool_expand[send_row], "mem", split_axis=0, concat_axis=0, tiled=True),
    )
    my_owner = lax.dynamic_index_in_dim(owner, group_index, 0, keepdims=False)
    my_rank = lax.dynamic_index_in_dim(rank, group_index, 0, keepdims=False)
    flat = my_owner * CAP + my_rank
    new_shrink = got_shrink.reshape((groups * CAP,) + got_shrink.shape[2:])[flat]
    new_expand = got_expand.reshape(groups * CAP, got_expand.shape[2])[flat]
    targets = evict_slots[0]
    slot_shrink = cache_shrink.at[targets].set(new_shrink)
    slot_expand = cache_expand.at[targets].set(new_expand)
    rows = activations.shape[0]
    nblocks = rows // BLOCK
    blocked = activations.reshape(nblocks, BLOCK, activations.shape[1])
    lowrank_state = jnp.einsum(
        "nbd,nrd->nbr", blocked, slot_shrink[block_slot], preferred_element_type=jnp.float32
    ).reshape(rows, -1)
    row_ids = jnp.arange(rows, dtype=jnp.int32)
    block_hot = (row_ids // BLOCK)[:, None] == jnp.arange(nblocks, dtype=jnp.int32)[None, :]
    row_slot = jnp.sum(jnp.where(block_hot, block_slot[None, :], 0), axis=1)
    row_live = row_ids % BLOCK < jnp.sum(jnp.where(block_hot, block_live_rows[None, :], 0), axis=1)
    slot_hot = row_slot[:, None] == jnp.arange(SLOTS, dtype=jnp.int32)[None, :]
    own = rows // tp_count
    start = lax.axis_index("tp") * own
    zero_value = jnp.zeros((), jnp.bfloat16)
    base_rows = lax.psum_scatter(
        jnp.dot(activations, base_weight, preferred_element_type=jnp.float32),
        "tp",
        scatter_dimension=0,
        tiled=True,
    )
    low_rows = lax.psum_scatter(lowrank_state, "tp", scatter_dimension=0, tiled=True).astype(
        jnp.bfloat16
    )
    full_expand = lax.all_gather(slot_expand, "tp", axis=1, tiled=True).reshape(-1, VALUE_FEATURES)
    own_hot = lax.dynamic_slice_in_dim(slot_hot, start, own, 0)
    chosen = jnp.where(own_hot[:, :, None], low_rows[:, None, :], zero_value).reshape(own, -1)
    total = base_rows + 0.5 * jnp.dot(chosen, full_expand, preferred_element_type=jnp.float32)
    own_live = lax.dynamic_slice_in_dim(row_live, start, own, 0)
    return jnp.where(own_live[:, None], total, 0.0).astype(jnp.bfloat16)


CHUNKS = 4
MESH = pl.DeviceIdType.MESH


def kernel(
    nm, nt, act_h, w_h, psh_h, pex_h, csh_h, cex_h, home_h, evict_h, eslot_h, bslot_h, live_h,
    out,
    home, evict, eslot, bslot, live, cx, hold, relay,
    act, w, psh, pst, allsh, alle, ssh, sex, xe, full, pf, own, sb, rb, slow, rlow,
    loc, int_sem, pex_sem, s_rel, r_rel, s_base, r_base, s_sh, r_sh, s_ex, r_ex, s_xe, r_xe, s_low, r_low,
):
    mm = lax.axis_index("mem")
    mt = lax.axis_index("tp")
    pool_dev = psh_h.shape[0]
    ranks = cex_h.shape[1] // VALUE_FEATURES
    near = mt + 1 - 2 * lax.rem(mt, 2)
    other = lax.rem(mt + 2, nt)
    far = nt - 1 - mt
    edge = (mt == 0) | (mt == nt - 1)
    inner = (mt > 0) & (mt < nt - 1)
    wide = w_h.shape[1] // CHUNKS

    barrier = pltpu.get_barrier_semaphore()
    for k in range(1, nt):
        pl.semaphore_signal(barrier, inc=1, device_id={"tp": lax.rem(mt + k, nt)}, device_id_type=MESH)
    for k in range(1, nm):
        pl.semaphore_signal(barrier, inc=1, device_id={"mem": lax.rem(mm + k, nm)}, device_id_type=MESH)

    load_int = []
    for n, (a, b) in enumerate(((home_h, home), (evict_h, evict), (eslot_h, eslot), (bslot_h, bslot), (live_h, live))):
        load_int.append(pltpu.make_async_copy(a, b, int_sem.at[n]))
    load_act = pltpu.make_async_copy(act_h, act, loc.at[0])
    load_act.start()
    load_w = []
    for c in range(CHUNKS):
        load_w.append(pltpu.make_async_copy(w_h.at[:, pl.ds(c * wide, wide)], w.at[c], loc.at[1 + c]))
    load_w[0].start()
    load_w[1].start()
    load_pex = []
    for r in range(ranks):
        load_pex.append(pltpu.make_async_copy(
            pex_h.at[:, pl.ds(r * VALUE_FEATURES, VALUE_FEATURES)],
            pst.at[pl.ds(r * pool_dev, pool_dev), :],
            pex_sem.at[r],
        ))
    load_psh = pltpu.make_async_copy(psh_h, psh, loc.at[5])
    load_csh = pltpu.make_async_copy(csh_h, allsh.at[pl.ds(0, SLOTS)], loc.at[6])
    load_cex = pltpu.make_async_copy(cex_h, cx, loc.at[7])

    def base_copy(c, peer, slot):
        return pltpu.make_async_remote_copy(
            src_ref=sb.at[c, peer], dst_ref=rb.at[c, slot],
            send_sem=s_base.at[c, peer], recv_sem=r_base.at[c, slot],
            device_id={"tp": peer}, device_id_type=MESH)

    def relay_copy(c):
        return pltpu.make_async_remote_copy(
            src_ref=sb.at[c, far], dst_ref=relay.at[c], send_sem=s_rel.at[c], recv_sem=r_rel.at[c],
            device_id={"tp": near}, device_id_type=MESH)

    def pair_copy(a, b, ss, rs, axis, peer, slot, base=0):
        return pltpu.make_async_remote_copy(
            src_ref=a.at[peer], dst_ref=b.at[base + slot],
            send_sem=ss.at[peer], recv_sem=rs.at[slot],
            device_id={axis: peer}, device_id_type=MESH)

    load_act.wait()
    for c in range(CHUNKS):
        load_w[c].wait()
        if c == 0:
            load_w[2].start()
            load_w[3].start()
            for copy in load_int + load_pex:
                copy.start()
        if c == 2:
            load_psh.start()
            load_csh.start()
            load_cex.start()
        pf[...] = jnp.dot(act[...], w[c], preferred_element_type=jnp.float32)
        if c == 0:
            pl.semaphore_wait(barrier, nt - 1 + nm - 1)

        def part(b):
            return pf[pl.ds(pl.multiple_of(b * BLOCK, BLOCK), BLOCK), :]

        sb[c, far] = part(far).astype(jnp.bfloat16)

        @pl.when(edge)
        def _():
            relay_copy(c).start()
            sb[c, other] = part(other).astype(jnp.bfloat16)
            base_copy(c, other, mt).start()

        @pl.when(inner)
        def _():
            base_copy(c, far, mt).start()
            hold[c] = part(other)

        sb[c, near] = part(near).astype(jnp.bfloat16)

        @pl.when(inner)
        def _():
            base_copy(c, near, mt).start()

        own[:, c * wide:(c + 1) * wide] = part(mt)

    @pl.when(edge)
    def _():
        for c in range(CHUNKS):
            base_copy(c, near, mt).start()

    for copy in load_int:
        copy.wait()

    def wanted(g):
        row = jnp.int32(0)
        for e in range(EVICT):
            h = home[evict[e, g]]
            o = lax.div(h, jnp.int32(pool_dev))
            row = jnp.where(o == mm, h - o * pool_dev, row)
        return row

    rows = [wanted(g) for g in range(nm)]
    shape = (nm * ranks, ranks * pool_dev)
    i = lax.broadcasted_iota(jnp.int32, shape, 0)
    q = lax.broadcasted_iota(jnp.int32, shape, 1)
    target = jnp.zeros(shape, jnp.int32)
    for g in range(nm):
        target = jnp.where((i >= g * ranks) & (i < (g + 1) * ranks), (i - g * ranks) * pool_dev + rows[g], target)
    hot = jnp.where(q == target, 1.0, 0.0).astype(jnp.bfloat16)
    for r in range(ranks):
        load_pex[r].wait()
    picked = jnp.dot(hot, pst[...], preferred_element_type=jnp.float32).astype(jnp.bfloat16)
    sex[...] = picked.reshape(nm, ranks, VALUE_FEATURES)
    for k in range(1, nm):
        pair_copy(sex, alle, s_ex, r_ex, "mem", lax.rem(mm + k, nm), mm, SLOTS).start()
    alle[SLOTS + mm] = sex[mm]
    @pl.when(inner)
    def _():
        for c in range(2):
            relay_copy(c).wait_recv()
            sb[c, other] = (hold[c] + relay[c].astype(jnp.float32)).astype(jnp.bfloat16)
            base_copy(c, other, mt).start()

    load_psh.wait()
    for k in range(1, nm):
        g = lax.rem(mm + k, nm)
        ssh[g] = psh[wanted(g)]
        pair_copy(ssh, allsh, s_sh, r_sh, "mem", g, mm, SLOTS).start()
    allsh[SLOTS + mm] = psh[wanted(mm)]

    owner = [lax.div(home[evict[e, mm]], jnp.int32(pool_dev)) for e in range(EVICT)]

    def place(b):
        c = bslot[b]
        index = c
        for e in range(EVICT):
            index = jnp.where(eslot[0, e] == c, SLOTS + owner[e], index)
        return index

    @pl.when(inner)
    def _():
        for c in range(2, CHUNKS):
            relay_copy(c).wait_recv()
            sb[c, other] = (hold[c] + relay[c].astype(jnp.float32)).astype(jnp.bfloat16)
            base_copy(c, other, mt).start()

    load_cex.wait()
    shape = (SLOTS * ranks, SLOTS)
    i = lax.broadcasted_iota(jnp.int32, shape, 0)
    q = lax.broadcasted_iota(jnp.int32, shape, 1)
    kept = jnp.zeros((SLOTS * ranks, VALUE_FEATURES), jnp.float32)
    for r in range(ranks):
        hot = jnp.where(i == q * ranks + r, 1.0, 0.0).astype(jnp.bfloat16)
        kept += jnp.dot(
            hot, cx[:, r * VALUE_FEATURES:(r + 1) * VALUE_FEATURES], preferred_element_type=jnp.float32)
    alle[0:SLOTS] = kept.astype(jnp.bfloat16).reshape(SLOTS, ranks, VALUE_FEATURES)
    for k in range(1, nm):
        pair_copy(sex, alle, s_ex, r_ex, "mem", lax.rem(mm + k, nm), lax.rem(mm + k, nm), SLOTS).wait_recv()
    for k in range(1, nt):
        peer = lax.rem(mt + k, nt)
        xe[peer] = alle[place(peer)]
        pair_copy(xe, full, s_xe, r_xe, "tp", peer, mt).start()
    full[mt] = alle[place(mt)]

    load_csh.wait()
    for k in range(1, nm):
        pair_copy(ssh, allsh, s_sh, r_sh, "mem", lax.rem(mm + k, nm), lax.rem(mm + k, nm), SLOTS).wait_recv()

    def low_of(b):
        return lax.dot_general(
            allsh[place(b)], act[pl.ds(pl.multiple_of(b * BLOCK, BLOCK), BLOCK), :],
            (((1,), (1,)), ((), ())), preferred_element_type=jnp.float32)

    for k in range(1, nt):
        peer = lax.rem(mt + k, nt)
        slow[peer] = low_of(peer)
        pair_copy(slow, rlow, s_low, r_low, "tp", peer, mt).start()
    low = low_of(mt)
    for k in range(1, nt):
        peer = lax.rem(mt + k, nt)
        pair_copy(xe, full, s_xe, r_xe, "tp", peer, peer).wait_recv()
        pair_copy(slow, rlow, s_low, r_low, "tp", peer, peer).wait_recv()
        low = low + rlow[peer]
    low = low.T.astype(jnp.bfloat16)
    here = lax.broadcasted_iota(jnp.int32, (BLOCK, wide), 0) < live[mt]

    @pl.when(inner)
    def _():
        for c in range(CHUNKS):
            base_copy(c, far, far).wait_recv()
            own[:, c * wide:(c + 1) * wide] += rb[c, far].astype(jnp.float32)

    for c in range(CHUNKS):
        cols = slice(c * wide, (c + 1) * wide)
        up = full[:, :, cols].reshape(nt * ranks, wide)
        total = own[:, cols] + 0.5 * jnp.dot(low, up, preferred_element_type=jnp.float32)
        for peer in (near, other):
            base_copy(c, peer, peer).wait_recv()
            total = total + rb[c, peer].astype(jnp.float32)
        out[:, cols] = jnp.where(here, total, 0.0).astype(jnp.bfloat16)

    for c in range(CHUNKS):
        base_copy(c, near, mt).wait_send()
        base_copy(c, other, mt).wait_send()

        @pl.when(edge)
        def _():
            relay_copy(c).wait_send()

        @pl.when(inner)
        def _():
            base_copy(c, far, mt).wait_send()

    for k in range(1, nt):
        peer = lax.rem(mt + k, nt)
        pair_copy(xe, full, s_xe, r_xe, "tp", peer, mt).wait_send()
        pair_copy(slow, rlow, s_low, r_low, "tp", peer, mt).wait_send()
    for k in range(1, nm):
        g = lax.rem(mm + k, nm)
        pair_copy(sex, alle, s_ex, r_ex, "mem", g, mm, SLOTS).wait_send()
        pair_copy(ssh, allsh, s_sh, r_sh, "mem", g, mm, SLOTS).wait_send()


def body(
    activations,
    base_weight,
    pool_shrink,
    pool_expand,
    cache_shrink,
    cache_expand,
    adapter_home,
    evict_adapters,
    evict_slots,
    block_slot,
    block_live_rows,
):
    nm, nt = lax.axis_size("mem"), lax.axis_size("tp")
    rows, depth = activations.shape
    ranks = pool_expand.shape[1] // VALUE_FEATURES
    if nt != 4 or rows != nt * BLOCK or ranks % 16 != 0:
        return plain_body(
            activations, base_weight, pool_shrink, pool_expand, cache_shrink, cache_expand,
            adapter_home, evict_adapters, evict_slots, block_slot, block_live_rows)
    pool_dev, rank = pool_shrink.shape[:2]
    wide = VALUE_FEATURES // CHUNKS
    bf, f32 = jnp.bfloat16, jnp.float32
    dma = pltpu.SemaphoreType.DMA
    any_spec = pl.BlockSpec(memory_space=pl.ANY)
    return pl.pallas_call(
        functools.partial(kernel, nm, nt),
        out_shape=jax.ShapeDtypeStruct((BLOCK, VALUE_FEATURES), bf),
        in_specs=[any_spec] * 11,
        out_specs=pl.BlockSpec(memory_space=pltpu.VMEM),
        scratch_shapes=[
            pltpu.SMEM(adapter_home.shape, jnp.int32),
            pltpu.SMEM(evict_adapters.shape[::-1], jnp.int32),
            pltpu.SMEM(evict_slots.shape, jnp.int32),
            pltpu.SMEM(block_slot.shape, jnp.int32),
            pltpu.SMEM(block_live_rows.shape, jnp.int32),
            pltpu.VMEM(cache_expand.shape, bf),
            pltpu.VMEM((CHUNKS, BLOCK, wide), f32),
            pltpu.VMEM((CHUNKS, BLOCK, wide), bf),
            pltpu.VMEM((rows, depth), bf),
            pltpu.VMEM((CHUNKS, depth, wide), bf),
            pltpu.VMEM((pool_dev, rank, depth), bf),
            pltpu.VMEM((ranks * pool_dev, VALUE_FEATURES), bf),
            pltpu.VMEM((SLOTS + nm, rank, depth), bf),
            pltpu.VMEM((SLOTS + nm, ranks, VALUE_FEATURES), bf),
            pltpu.VMEM((nm, rank, depth), bf),
            pltpu.VMEM((nm, ranks, VALUE_FEATURES), bf),
            pltpu.VMEM((nt, ranks, VALUE_FEATURES), bf),
            pltpu.VMEM((nt, ranks, VALUE_FEATURES), bf),
            pltpu.VMEM((rows, wide), f32),
            pltpu.VMEM((BLOCK, VALUE_FEATURES), f32),
            pltpu.VMEM((CHUNKS, nt, BLOCK, wide), bf),
            pltpu.VMEM((CHUNKS, nt, BLOCK, wide), bf),
            pltpu.VMEM((nt, rank, BLOCK), f32),
            pltpu.VMEM((nt, rank, BLOCK), f32),
            dma((8,)),
            dma((5,)),
            dma((ranks,)),
            dma((CHUNKS,)), dma((CHUNKS,)),
            dma((CHUNKS, nt)), dma((CHUNKS, nt)),
            dma((nm,)), dma((nm,)),
            dma((nm,)), dma((nm,)),
            dma((nt,)), dma((nt,)),
            dma((nt,)), dma((nt,)),
        ],
        compiler_params=pltpu.CompilerParams(
            collective_id=0, has_side_effects=True, vmem_limit_bytes=60 * 1024 * 1024),
        cost_estimate=pl.CostEstimate(
            flops=2 * rows * depth * (VALUE_FEATURES + rank), bytes_accessed=16 * 1024 * 1024, transcendentals=0),
    )(
        activations, base_weight, pool_shrink, pool_expand, cache_shrink,
        cache_expand,
        adapter_home, evict_adapters.T, evict_slots, block_slot, block_live_rows,
    )


def solution(mesh):
    placed = (
        P(("rep", "mem"), "tp"),
        P("tp", None),
        P("mem", None, "tp"),
        P("mem", "tp"),
        P(("rep", "mem"), None, "tp"),
        P(("rep", "mem"), "tp"),
        P("rep"),
        P("rep", None),
        P(("rep", "mem"), None),
        P(("rep", "mem")),
        P(("rep", "mem")),
    )
    return jax.shard_map(
        body, mesh=mesh, in_specs=placed, out_specs=P(("rep", "mem", "tp"), None), check_vma=False
    )
```
